128 devices in a mesh: tp: 16 (over x, z_lo, core), dp: 8 (over y, z_hi).
Axes of the slice: x: 4, y: 4, z: 4 (z_hi: 2, z_lo: 2; z = z_hi * 2 + z_lo), core: 2. Of those that a mesh axis runs over, the one named last changes fastest.
Arguments:
- grad_out: bfloat16 [7168, 8192], P(('dp', 'tp')), may hold values from -6 to 6
- gate_act: bfloat16 [7168, 14336], P('dp', 'tp'), may hold values from -8 to 8
- up_act: bfloat16 [7168, 14336], P('dp', 'tp'), may hold values from -6 to 6
- down_weight: bfloat16 [14336, 8192], P('tp'), may hold values from -0.0625 to 0.0625
Outputs:
- grad_gate: bfloat16 [7168, 14336], P('dp', 'tp')
- grad_up: bfloat16 [7168, 14336], P('dp', 'tp')
- grad_down: bfloat16 [14336, 8192], P(('tp', 'dp'))
The draws below stay inside these ranges and needn't reach their ends.
All inputs are finite; a program needn't handle non-finite values.
Results may differ from the reference program's by a relative error of at most 0.013.
Values may be sent and summed in bfloat16 or wider, within the bound.
A program may use at most 128 MiB of HBM per device.

```python
import math
import jax
import jax.numpy as jnp
from jax import lax

D = 8192
FF = 14336
GROUP = 896
TOKENS = 7168
N_DP = 8


def block_scale(stream_key, extent, shards, low, high):
    def one(axis_at, shards_of):
        draws = jax.random.uniform(jax.random.fold_in(jax.random.fold_in(stream_key, 6), axis_at), (shards_of,), jnp.float32, low / len(shards), high / len(shards))
        return jnp.repeat(jnp.exp(draws), extent[axis_at] // shards_of).reshape((-1,) + (1,) * (len(extent) - axis_at - 1))

    gain = one(*shards[0])
    for cut in shards[1:]:
        gain = gain * one(*cut)
    return gain


def gaussian(own_key, dims, width, limit, shards=(), dtype=jnp.bfloat16):
    array = jax.random.normal(own_key, dims, jnp.float32) * width
    if len(shards) > 0:
        array = block_scale(own_key, dims, shards, -0.22, 0.18) * array
    return jnp.clip(array, min=-limit, max=limit).astype(dtype)


def setup_inputs(seed: int = 0) -> dict:
    keys = jax.random.split(jax.random.key(seed), 5)
    return {
        "grad_out": gaussian(keys[0], (TOKENS, D), 1.0, 6.0, ((0, 128),)),
        "gate_act": gaussian(keys[1], (TOKENS, FF), 1.5, 8.0, ((0, 8), (1, 16))),
        "up_act": gaussian(keys[2], (TOKENS, FF), 1.0, 6.0, ((0, 8), (1, 16))),
        "down_weight": gaussian(keys[3], (FF, D), D ** -0.5, 0.0625, ((0, 16),)),
    }


def reference(grad_out, gate_act, up_act, down_weight):
    gate_val = gate_act.astype(jnp.float32)
    up_val = up_act.astype(jnp.float32)
    squash = jax.nn.sigmoid(gate_val)
    hidden = (gate_val * squash * up_val).astype(jnp.bfloat16)
    grad_hidden = jnp.dot(grad_out, down_weight.T, preferred_element_type=jnp.float32)
    grad_gate = (grad_hidden * up_val * squash * (1.0 + gate_val * (1.0 - squash))).astype(jnp.bfloat16)
    grad_up = (grad_hidden * gate_val * squash).astype(jnp.bfloat16)
    hid_groups = hidden.reshape(N_DP, GROUP, FF)
    out_groups = grad_out.reshape(N_DP, GROUP, D)

    def add_group(running, pair):
        partial_value = jnp.dot(pair[0].T, pair[1], preferred_element_type=jnp.float32).astype(jnp.bfloat16)
        partial_value = lax.optimization_barrier(partial_value)
        return (running + partial_value.astype(jnp.float32), None)
    running, unused = lax.scan(add_group, jnp.zeros((FF, D), jnp.float32), (hid_groups, out_groups))
    grad_scale = 1.0 / math.sqrt(TOKENS)
    grad_down = (running * grad_scale).astype(jnp.bfloat16)
    return (grad_gate, grad_up, grad_down)
```

```python
import functools
import math

import jax
import jax.numpy as jnp
from jax import lax
from jax.experimental import pallas as pl
from jax.experimental.pallas import tpu as pltpu
from jax.sharding import PartitionSpec as P

MESH = pl.DeviceIdType.MESH
D = 8192
FF = 896
GROUP = 896
CHUNK = 112
SLICES = 16
W = D // 2 // SLICES
HALF = D // 2
MSGS = 15
BLK = 128
DEPTH = 8


def kernel(scale, go_ref, gate_ref, up_ref, w_ref, gg_ref, gu_ref, gd_ref,
           g, ht, ho, gate, up, acc, wbuf, part, ra, rb, rc, mine, theirs, gd,
           ss, rs, hs, hr, ls, lr, wsem, lsem, osem):
    tp, dp = lax.axis_index("tp"), lax.axis_index("dp")
    x, y, c = tp // 4, dp // 2, tp % 2
    zh, zl = dp % 2, (tp // 2) % 2
    z = zh * 2 + zl
    f32 = jnp.float32

    def at(xx, yy, zz, cc):
        return {"dp": yy * 2 + zz // 2, "tp": xx * 4 + (zz % 2) * 2 + cc}

    def kind(k):
        return jnp.where((k % 2 == 0) & (k >= 2), 1, 0)

    def pq(k):
        b = kind(k)
        return x + b * (z - x), z + b * (x - z)

    def q_dev(k, d):
        b = kind(k)
        return at((x + b * d + 4) % 4, y, (z + (1 - b) * d + 4) % 4, c)

    def p_dev(k, d):
        b = kind(k)
        return at((x + (1 - b) * d + 4) % 4, y, (z + b * d + 4) % 4, c)

    def y_dev(d):
        return at(x, (y + d + 4) % 4, z, c)

    sib = at(x, y, z, 1 - c)
    partner = at(x, y, (z + 2) % 4, c)

    def rcopy(ref, k, m, dev):
        return pltpu.make_async_remote_copy(
            src_ref=ref, dst_ref=ref, send_sem=ss.at[k, m], recv_sem=rs.at[k, m],
            device_id=dev, device_id_type=MESH)

    def one(h, k, p, q):
        return g.at[h, k, pl.ds(((p + 4) % 4) * 4 + (q + 4) % 4, 1)]

    def group(h, k, p):
        return g.at[h, k, pl.ds(((p + 4) % 4) * 4, 4)]

    def half(h, k, p, j):
        return g.at[h, k, pl.ds(((p + 4) % 4) * 4 + 2 * j, 2)]

    def sgn(k):
        return 1 - 2 * ((k // 2) % 2)

    def ysgn(k):
        return 1 - 2 * (k % 2)

    cp_gate = pltpu.make_async_copy(gate_ref, gate, lsem.at[0])
    cp_up = pltpu.make_async_copy(up_ref, up, lsem.at[1])
    cp_mine = pltpu.make_async_copy(go_ref.at[:, pl.ds(pl.multiple_of(c * HALF, HALF), HALF)], mine, lsem.at[2])
    cp_mine.start()
    cp_gate.start()
    cp_up.start()

    barrier = pltpu.get_barrier_semaphore()
    for dev in (at((x + 1) % 4, y, z, c), at((x + 3) % 4, y, z, c), at(x, y, (z + 1) % 4, c),
                at(x, y, (z + 3) % 4, c), y_dev(1), y_dev(-1), sib, partner):
        pl.semaphore_signal(barrier, inc=1, device_id=dev, device_id_type=MESH)
    pl.semaphore_wait(barrier, 8)

    cp_sib = pltpu.make_async_remote_copy(
        src_ref=go_ref.at[:, pl.ds(pl.multiple_of((1 - c) * HALF, HALF), HALF)], dst_ref=theirs,
        send_sem=ls.at[0], recv_sem=lr.at[0], device_id=sib, device_id_type=MESH)
    cp_sib.start()
    acc[...] = jnp.zeros_like(acc)
    cp_mine.wait()
    cp_sib.wait()

    cp_hid = pltpu.make_async_remote_copy(
        src_ref=ht.at[:, 1 - zh], dst_ref=ho, send_sem=hs.at[0], recv_sem=hr.at[0],
        device_id=partner, device_id_type=MESH)

    def w_copy(k, h):
        cols = pl.ds(pl.multiple_of(h * HALF + k * W, W), W)
        return pltpu.make_async_copy(w_ref.at[:, cols], wbuf.at[k % 3, h], wsem.at[k % 3, h])

    def e1(k):
        p, q = pq(k)
        cols = pl.ds(pl.multiple_of(k * W, W), W)
        a, b = mine[:, cols], theirs[:, cols]
        first, last = jnp.where(c == 0, a, b), jnp.where(c == 0, b, a)
        g[c, k, p * 4 + q] = jnp.concatenate([first, last], axis=0)
        rcopy(one(c, k, p, q), k, 0, q_dev(k, 1)).start()
        rcopy(one(c, k, p, q), k, 1, q_dev(k, -1)).start()

    def e2(k):
        p, q = pq(k)
        rcopy(one(c, k, p, q - 1), k, 0, q_dev(k, 1)).wait_recv()
        rcopy(one(c, k, p, q + 1), k, 1, q_dev(k, 1)).wait_recv()
        s = sgn(k)
        rcopy(one(c, k, p, q - s), k, 2, q_dev(k, s)).start()

    def e3(k):
        p, q = pq(k)
        rcopy(one(c, k, p, q + 2), k, 2, q_dev(k, 1)).wait_recv()
        rcopy(group(c, k, p), k, 3, p_dev(k, 1)).start()
        rcopy(group(c, k, p), k, 4, p_dev(k, -1)).start()
        rcopy(group(c, k, p), k, 7, sib).start()

    def e4(k):
        p, q = pq(k)
        rcopy(group(c, k, p - 1), k, 3, p_dev(k, 1)).wait_recv()
        rcopy(half(c, k, p - 1, 0), k, 5, p_dev(k, 1)).start()
        rcopy(group(c, k, p - 1), k, 8, sib).start()
        rcopy(group(c, k, p + 1), k, 4, p_dev(k, 1)).wait_recv()
        rcopy(half(c, k, p + 1, 1), k, 6, p_dev(k, -1)).start()
        rcopy(group(c, k, p + 1), k, 9, sib).start()
        for h in range(2):
            w_copy(k, h).start()

    def e5(k):
        p, q = pq(k)
        rcopy(half(c, k, p + 2, 0), k, 5, p_dev(k, 1)).wait_recv()
        rcopy(half(c, k, p + 2, 0), k, 10, sib).start()
        rcopy(half(c, k, p + 2, 1), k, 6, p_dev(k, 1)).wait_recv()
        rcopy(half(c, k, p + 2, 1), k, 11, sib).start()

    def rows(h, k, zz):
        b = kind(k)
        blocks = []
        for j in range(8):
            xj, zj = j // 2, zz * 2 + j % 2
            pos = (1 - b) * (xj * 4 + zj) + b * (zj * 4 + xj)
            blocks.append(g[h, k, pos])
        return jnp.concatenate(blocks, axis=0)

    def y_copy(k, src, dst, m, d):
        return pltpu.make_async_remote_copy(
            src_ref=src, dst_ref=dst, send_sem=ss.at[k, m], recv_sem=rs.at[k, m],
            device_id=y_dev(d), device_id_type=MESH)

    def blk(k, d):
        return part.at[k, (y + d + 4) % 4]

    def e6(k):
        p, q = pq(k)
        rcopy(group(1 - c, k, p), k, 7, sib).wait_recv()
        rcopy(group(1 - c, k, p - 1), k, 8, sib).wait_recv()
        rcopy(group(1 - c, k, p + 1), k, 9, sib).wait_recv()
        rcopy(half(1 - c, k, p + 2, 0), k, 10, sib).wait_recv()
        rcopy(half(1 - c, k, p + 2, 1), k, 11, sib).wait_recv()
        for h in range(2):
            own = ht[:, zh].reshape(FF // 2, GROUP)
            dw = jnp.dot(own, rows(h, k, zh), preferred_element_type=f32)
            dw += jnp.dot(ho[...].reshape(FF // 2, GROUP), rows(h, k, 1 - zh), preferred_element_type=f32)
            part[k, :, :, h * W:(h + 1) * W] = dw.astype(jnp.bfloat16).reshape(4, CHUNK, W)
        s = ysgn(k)
        y_copy(k, blk(k, 2), ra.at[k], 12, s).start()
        y_copy(k, blk(k, -s), rc.at[k], 14, -s).start()

    def e6b(k):
        for h in range(2):
            w_copy(k, h).wait()
        total = acc[...]
        for h in range(2):
            total += lax.dot_general(rows(h, k, zh), wbuf[k % 3, h], (((1,), (1,)), ((), ())),
                                     preferred_element_type=f32)
        acc[...] = total

    def e7(k):
        s = ysgn(k)
        y_copy(k, blk(k, 2), ra.at[k], 12, s).wait_recv()
        mid = (y + s + 4) % 4
        part[k, mid] = (part[k, mid].astype(f32) + ra[k].astype(f32)).astype(jnp.bfloat16)
        y_copy(k, blk(k, s), rb.at[k], 13, s).start()

    def e8(k):
        s = ysgn(k)
        p, q = pq(k)
        y_copy(k, blk(k, s), rb.at[k], 13, s).wait_recv()
        y_copy(k, blk(k, -s), rc.at[k], 14, -s).wait_recv()
        total = part[k, y].astype(f32) + rb[k].astype(f32) + rc[k].astype(f32)
        total = (total * scale).astype(jnp.bfloat16)
        for h in range(2):
            gd[:, pl.ds(pl.multiple_of(h * HALF + k * W, W), W)] = total[:, h * W:(h + 1) * W]
        rcopy(one(c, k, p, q), k, 0, sib).wait_send()
        rcopy(one(c, k, p, q), k, 1, sib).wait_send()
        rcopy(one(c, k, p, q - sgn(k)), k, 2, sib).wait_send()
        rcopy(group(c, k, p), k, 3, sib).wait_send()
        rcopy(group(c, k, p), k, 4, sib).wait_send()
        rcopy(half(c, k, p - 1, 0), k, 5, sib).wait_send()
        rcopy(half(c, k, p + 1, 1), k, 6, sib).wait_send()
        rcopy(group(c, k, p), k, 7, sib).wait_send()
        rcopy(group(c, k, p - 1), k, 8, sib).wait_send()
        rcopy(group(c, k, p + 1), k, 9, sib).wait_send()
        rcopy(half(c, k, p + 2, 0), k, 10, sib).wait_send()
        rcopy(half(c, k, p + 2, 1), k, 11, sib).wait_send()
        y_copy(k, blk(k, 2), ra.at[k], 12, s).wait_send()
        y_copy(k, blk(k, s), rb.at[k], 13, s).wait_send()
        y_copy(k, blk(k, -s), rc.at[k], 14, -s).wait_send()

    def hidden_block(t):
        at_t = pl.ds(pl.multiple_of(t * BLK, BLK), BLK)
        gv, uv = gate[at_t, :].astype(f32), up[at_t, :].astype(f32)
        hid = (gv * jax.nn.sigmoid(gv) * uv).T.astype(jnp.bfloat16)
        ht[:, :, :, at_t] = hid.reshape(4, 2, CHUNK, BLK)

    def step(i, carry):
        def stage(off, fn):
            k = i - off

            @pl.when((k >= 0) & (k < SLICES))
            def _():
                fn(k)

        stage(2, e3)
        stage(1, e2)
        stage(0, e1)

        @pl.when(i == 0)
        def _():
            cp_gate.wait()
            cp_up.wait()

        @pl.when(i < 4)
        def _():
            hidden_block(2 * i)

        @pl.when(i < 3)
        def _():
            hidden_block(2 * i + 1)

        @pl.when(i == 3)
        def _():
            cp_hid.start()

        stage(4, e4)
        stage(5, e5)

        @pl.when(i == 6)
        def _():
            cp_hid.wait()

        stage(6, e6)
        stage(7, e7)
        stage(6, e6b)
        stage(8, e8)
        return carry

    lax.fori_loop(0, SLICES + DEPTH, step, 0)

    cp_gd = pltpu.make_async_copy(gd, gd_ref, osem.at[0])
    cp_gd.start()

    def finish(t, carry):
        at_t = pl.ds(pl.multiple_of(t * BLK, BLK), BLK)
        gv, uv, gh = gate[at_t, :].astype(f32), up[at_t, :].astype(f32), acc[at_t, :]
        sq = jax.nn.sigmoid(gv)
        gate[at_t, :] = (gh * uv * sq * (1.0 + gv * (1.0 - sq))).astype(jnp.bfloat16)
        up[at_t, :] = (gh * gv * sq).astype(jnp.bfloat16)
        return carry

    lax.fori_loop(0, GROUP // BLK, finish, 0)
    cp_gg = pltpu.make_async_copy(gate, gg_ref, osem.at[1])
    cp_gu = pltpu.make_async_copy(up, gu_ref, osem.at[2])
    cp_gg.start()
    cp_gu.start()
    cp_gd.wait()
    cp_gg.wait()
    cp_gu.wait()


def body(grad_out, gate_act, up_act, down_weight):
    token_total = grad_out.shape[0] * lax.axis_size("tp") * lax.axis_size("dp")
    bf16 = jnp.bfloat16
    any_spec = pl.BlockSpec(memory_space=pl.ANY)
    dma = pltpu.SemaphoreType.DMA
    return pl.pallas_call(
        functools.partial(kernel, 1.0 / math.sqrt(token_total)),
        out_shape=(jax.ShapeDtypeStruct((GROUP, FF), bf16), jax.ShapeDtypeStruct((GROUP, FF), bf16),
                   jax.ShapeDtypeStruct((CHUNK, D), bf16)),
        in_specs=[any_spec] * 4,
        out_specs=(any_spec,) * 3,
        scratch_shapes=[
            pltpu.VMEM((2, SLICES, 16, CHUNK, W), bf16),
            pltpu.VMEM((4, 2, CHUNK, GROUP), bf16),
            pltpu.VMEM((4, CHUNK, GROUP), bf16),
            pltpu.VMEM((GROUP, FF), bf16),
            pltpu.VMEM((GROUP, FF), bf16),
            pltpu.VMEM((GROUP, FF), jnp.float32),
            pltpu.VMEM((3, 2, FF, W), bf16),
            pltpu.VMEM((SLICES, 4, CHUNK, 2 * W), bf16),
            pltpu.VMEM((SLICES, CHUNK, 2 * W), bf16),
            pltpu.VMEM((SLICES, CHUNK, 2 * W), bf16),
            pltpu.VMEM((SLICES, CHUNK, 2 * W), bf16),
            pltpu.VMEM((CHUNK // 2, HALF), bf16),
            pltpu.VMEM((CHUNK // 2, HALF), bf16),
            pltpu.VMEM((CHUNK, D), bf16),
            dma((SLICES, MSGS)), dma((SLICES, MSGS)),
            dma((1,)), dma((1,)), dma((1,)), dma((1,)),
            dma((3, 2)), dma((3,)), dma((3,)),
        ],
        compiler_params=pltpu.CompilerParams(
            collective_id=0, has_side_effects=True, vmem_limit_bytes=62 * 1024 * 1024),
        cost_estimate=pl.CostEstimate(flops=4 * FF * GROUP * D, bytes_accessed=24 * 1024 * 1024,
                                      transcendentals=GROUP * FF * 2),
    )(grad_out, gate_act, up_act, down_weight)


def solution(mesh):
    return jax.shard_map(
        body,
        mesh=mesh,
        in_specs=(P(("dp", "tp"), None), P("dp", "tp"), P("dp", "tp"), P("tp", None)),
        out_specs=(P("dp", "tp"), P("dp", "tp"), P(("tp", "dp"), None)),
        check_vma=False,
    )
```

```python
import functools
import math

import jax
import jax.numpy as jnp
from jax import lax
from jax.experimental import pallas as pl
from jax.experimental.pallas import tpu as pltpu
from jax.sharding import PartitionSpec as P

MESH = pl.DeviceIdType.MESH
D = 8192
FF = 896
GROUP = 896
CHUNK = 112
SLICES = 16
TAIL = 2
W = D // 2 // SLICES
HALF = D // 2
MSGS = 15
BLK = 128
BLOCKS = GROUP // BLK
HID_PER = 1
FIN_PER = 3
O1, O2, O3, O4, O5, O6, O6B, O7, O8 = 0, 2, 4, 6, 8, 9, 9, 10, 11


def kernel(scale, go_ref, gate_ref, up_ref, w_ref, gg_ref, gu_ref, gd_ref,
           g, ht, ho, gate, up, acc, wbuf, part, ra, rb, rc, mine, theirs, gd,
           ss, rs, hs, hr, ls, lr, wsem, lsem, osem):
    tp, dp = lax.axis_index("tp"), lax.axis_index("dp")
    x, y, c = tp // 4, dp // 2, tp % 2
    zh, zl = dp % 2, (tp // 2) % 2
    z = zh * 2 + zl
    f32 = jnp.float32

    def at(xx, yy, zz, cc):
        return {"dp": yy * 2 + zz // 2, "tp": xx * 4 + (zz % 2) * 2 + cc}

    def kind(k):
        return jnp.where((k % 2 == 0) & (k >= 2), 1, 0)

    def pq(k):
        b = kind(k)
        return x + b * (z - x), z + b * (x - z)

    def q_dev(k, d):
        b = kind(k)
        return at((x + b * d + 4) % 4, y, (z + (1 - b) * d + 4) % 4, c)

    def p_dev(k, d):
        b = kind(k)
        return at((x + (1 - b) * d + 4) % 4, y, (z + b * d + 4) % 4, c)

    def y_dev(d):
        return at(x, (y + d + 4) % 4, z, c)

    sib = at(x, y, z, 1 - c)
    partner = at(x, y, (z + 2) % 4, c)

    def rcopy(ref, k, m, dev):
        return pltpu.make_async_remote_copy(
            src_ref=ref, dst_ref=ref, send_sem=ss.at[k, m], recv_sem=rs.at[k, m],
            device_id=dev, device_id_type=MESH)

    def one(h, k, p, q):
        return g.at[h, k, pl.ds(((p + 4) % 4) * 4 + (q + 4) % 4, 1)]

    def group(h, k, p):
        return g.at[h, k, pl.ds(((p + 4) % 4) * 4, 4)]

    def half(h, k, p, j):
        return g.at[h, k, pl.ds(((p + 4) % 4) * 4 + 2 * j, 2)]

    def sgn(k):
        return 1 - 2 * ((k // 2) % 2)

    def ysgn(k):
        return 1 - 2 * (k % 2)

    cp_gate = pltpu.make_async_copy(gate_ref, gate, lsem.at[0])
    cp_up = pltpu.make_async_copy(up_ref, up, lsem.at[1])
    cp_mine = pltpu.make_async_copy(go_ref.at[:, pl.ds(pl.multiple_of(c * HALF, HALF), HALF)], mine, lsem.at[2])
    cp_mine.start()
    cp_gate.start()
    cp_up.start()

    barrier = pltpu.get_barrier_semaphore()
    for dev in (at((x + 1) % 4, y, z, c), at((x + 3) % 4, y, z, c), at(x, y, (z + 1) % 4, c),
                at(x, y, (z + 3) % 4, c), y_dev(1), y_dev(-1), y_dev(2), sib, partner):
        pl.semaphore_signal(barrier, inc=1, device_id=dev, device_id_type=MESH)
    pl.semaphore_wait(barrier, 9)

    cp_sib = pltpu.make_async_remote_copy(
        src_ref=go_ref.at[:, pl.ds(pl.multiple_of((1 - c) * HALF, HALF), HALF)], dst_ref=theirs,
        send_sem=ls.at[0], recv_sem=lr.at[0], device_id=sib, device_id_type=MESH)
    cp_sib.start()
    acc[...] = jnp.zeros_like(acc)
    cp_mine.wait()
    cp_sib.wait()

    def hid_copy(t):
        at_t = pl.ds(pl.multiple_of(t * BLK, BLK), BLK)
        return pltpu.make_async_remote_copy(
            src_ref=ht.at[:, 1 - zh, :, at_t], dst_ref=ho.at[:, :, at_t],
            send_sem=hs.at[t], recv_sem=hr.at[t], device_id=partner, device_id_type=MESH)

    def w_copy(k, h):
        cols = pl.ds(pl.multiple_of(h * HALF + k * W, W), W)
        return pltpu.make_async_copy(w_ref.at[:, cols], wbuf.at[k % 3, h], wsem.at[k % 3, h])

    def w_start(k):
        for h in range(2):
            w_copy(k, h).start()

    def e1(k):
        p, q = pq(k)
        cols = pl.ds(pl.multiple_of(k * W, W), W)
        a, b = mine[:, cols], theirs[:, cols]
        first, last = jnp.where(c == 0, a, b), jnp.where(c == 0, b, a)
        g[c, k, p * 4 + q] = jnp.concatenate([first, last], axis=0)
        rcopy(one(c, k, p, q), k, 0, q_dev(k, 1)).start()
        rcopy(one(c, k, p, q), k, 1, q_dev(k, -1)).start()

    def e2(k):
        p, q = pq(k)
        rcopy(one(c, k, p, q - 1), k, 0, q_dev(k, 1)).wait_recv()
        rcopy(one(c, k, p, q + 1), k, 1, q_dev(k, 1)).wait_recv()
        s = sgn(k)
        rcopy(one(c, k, p, q - s), k, 2, q_dev(k, s)).start()

    def e3(k):
        p, q = pq(k)
        rcopy(one(c, k, p, q + 2), k, 2, q_dev(k, 1)).wait_recv()
        rcopy(group(c, k, p), k, 3, p_dev(k, 1)).start()
        rcopy(group(c, k, p), k, 4, p_dev(k, -1)).start()
        rcopy(group(c, k, p), k, 7, sib).start()

    def e4(k):
        p, q = pq(k)
        rcopy(group(c, k, p - 1), k, 3, p_dev(k, 1)).wait_recv()
        rcopy(half(c, k, p - 1, 0), k, 5, p_dev(k, 1)).start()
        rcopy(group(c, k, p - 1), k, 8, sib).start()
        rcopy(group(c, k, p + 1), k, 4, p_dev(k, 1)).wait_recv()
        rcopy(half(c, k, p + 1, 1), k, 6, p_dev(k, -1)).start()
        rcopy(group(c, k, p + 1), k, 9, sib).start()

    def e5(k):
        p, q = pq(k)
        rcopy(half(c, k, p + 2, 0), k, 5, p_dev(k, 1)).wait_recv()
        rcopy(half(c, k, p + 2, 0), k, 10, sib).start()
        rcopy(half(c, k, p + 2, 1), k, 6, p_dev(k, 1)).wait_recv()
        rcopy(half(c, k, p + 2, 1), k, 11, sib).start()

    def rows(h, k, zz):
        b = kind(k)
        blocks = []
        for j in range(8):
            xj, zj = j // 2, zz * 2 + j % 2
            pos = (1 - b) * (xj * 4 + zj) + b * (zj * 4 + xj)
            blocks.append(g[h, k, pos])
        return jnp.concatenate(blocks, axis=0)

    def y_copy(k, src, dst, m, d):
        return pltpu.make_async_remote_copy(
            src_ref=src, dst_ref=dst, send_sem=ss.at[k, m], recv_sem=rs.at[k, m],
            device_id=y_dev(d), device_id_type=MESH)

    def blk(k, d):
        return part.at[k, (y + d + 4) % 4]

    def e6(k):
        p, q = pq(k)
        rcopy(group(1 - c, k, p), k, 7, sib).wait_recv()
        rcopy(group(1 - c, k, p - 1), k, 8, sib).wait_recv()
        rcopy(group(1 - c, k, p + 1), k, 9, sib).wait_recv()
        rcopy(half(1 - c, k, p + 2, 0), k, 10, sib).wait_recv()
        rcopy(half(1 - c, k, p + 2, 1), k, 11, sib).wait_recv()
        for h in range(2):
            own = ht[:, zh].reshape(FF // 2, GROUP)
            dw = jnp.dot(own, rows(h, k, zh), preferred_element_type=f32)
            dw += jnp.dot(ho[...].reshape(FF // 2, GROUP), rows(h, k, 1 - zh), preferred_element_type=f32)
            part[k, :, :, h * W:(h + 1) * W] = dw.astype(jnp.bfloat16).reshape(4, CHUNK, W)
        s = ysgn(k)
        y_copy(k, blk(k, 2), ra.at[k], 12, jnp.where(k < SLICES - TAIL, s, 2)).start()
        y_copy(k, blk(k, -s), rc.at[k], 14, -s).start()

        @pl.when(k >= SLICES - TAIL)
        def _():
            y_copy(k, blk(k, s), rb.at[k], 13, s).start()

    def e6b(k):
        for h in range(2):
            w_copy(k, h).wait()
        total = acc[...]
        for h in range(2):
            total += lax.dot_general(rows(h, k, zh), wbuf[k % 3, h], (((1,), (1,)), ((), ())),
                                     preferred_element_type=f32)
        acc[...] = total

    def e7(k):
        s = ysgn(k)

        @pl.when(k < SLICES - TAIL)
        def _():
            y_copy(k, blk(k, 2), ra.at[k], 12, s).wait_recv()
            mid = (y + s + 4) % 4
            part[k, mid] = (part[k, mid].astype(f32) + ra[k].astype(f32)).astype(jnp.bfloat16)
            y_copy(k, blk(k, s), rb.at[k], 13, s).start()

    def e8(k):
        s = ysgn(k)
        p, q = pq(k)
        y_copy(k, blk(k, s), rb.at[k], 13, s).wait_recv()
        y_copy(k, blk(k, -s), rc.at[k], 14, -s).wait_recv()
        total = part[k, y].astype(f32) + rb[k].astype(f32) + rc[k].astype(f32)

        def put(total):
            total = (total * scale).astype(jnp.bfloat16)
            for h in range(2):
                gd[:, pl.ds(pl.multiple_of(h * HALF + k * W, W), W)] = total[:, h * W:(h + 1) * W]

        @pl.when(k < SLICES - TAIL)
        def _():
            put(total)

        @pl.when(k >= SLICES - TAIL)
        def _():
            y_copy(k, blk(k, 2), ra.at[k], 12, 2).wait_recv()
            put(total + ra[k].astype(f32))

        rcopy(one(c, k, p, q), k, 0, sib).wait_send()
        rcopy(one(c, k, p, q), k, 1, sib).wait_send()
        rcopy(one(c, k, p, q - sgn(k)), k, 2, sib).wait_send()
        rcopy(group(c, k, p), k, 3, sib).wait_send()
        rcopy(group(c, k, p), k, 4, sib).wait_send()
        rcopy(half(c, k, p - 1, 0), k, 5, sib).wait_send()
        rcopy(half(c, k, p + 1, 1), k, 6, sib).wait_send()
        rcopy(group(c, k, p), k, 7, sib).wait_send()
        rcopy(group(c, k, p - 1), k, 8, sib).wait_send()
        rcopy(group(c, k, p + 1), k, 9, sib).wait_send()
        rcopy(half(c, k, p + 2, 0), k, 10, sib).wait_send()
        rcopy(half(c, k, p + 2, 1), k, 11, sib).wait_send()
        y_copy(k, blk(k, 2), ra.at[k], 12, s).wait_send()
        y_copy(k, blk(k, s), rb.at[k], 13, s).wait_send()
        y_copy(k, blk(k, -s), rc.at[k], 14, -s).wait_send()

    def hidden_block(t):
        at_t = pl.ds(pl.multiple_of(t * BLK, BLK), BLK)
        gv, uv = gate[at_t, :].astype(f32), up[at_t, :].astype(f32)
        hid = (gv * jax.nn.sigmoid(gv) * uv).T.astype(jnp.bfloat16)
        ht[:, :, :, at_t] = hid.reshape(4, 2, CHUNK, BLK)
        hid_copy(t).start()

    def out_copies(t):
        at_t = pl.ds(pl.multiple_of(t * BLK, BLK), BLK)
        return (pltpu.make_async_copy(gate.at[at_t, :], gg_ref.at[at_t, :], osem.at[1, t]),
                pltpu.make_async_copy(up.at[at_t, :], gu_ref.at[at_t, :], osem.at[2, t]))

    def finish(t):
        at_t = pl.ds(pl.multiple_of(t * BLK, BLK), BLK)
        gv, uv, gh = gate[at_t, :].astype(f32), up[at_t, :].astype(f32), acc[at_t, :]
        sq = jax.nn.sigmoid(gv)
        gate[at_t, :] = (gh * uv * sq * (1.0 + gv * (1.0 - sq))).astype(jnp.bfloat16)
        up[at_t, :] = (gh * gv * sq).astype(jnp.bfloat16)
        for cp in out_copies(t):
            cp.start()

    def step(i, carry):
        def stage(off, fn):
            k = i - off

            @pl.when((k >= 0) & (k < SLICES))
            def _():
                fn(k)

        stage(O3, e3)
        stage(O2, e2)
        stage(O1, e1)

        @pl.when(i == 0)
        def _():
            cp_gate.wait()
            cp_up.wait()

        for b in range(HID_PER):
            t = i * HID_PER + b

            @pl.when(t < BLOCKS)
            def _():
                hidden_block(t)

        stage(O4, e4)
        stage(O5, e5)

        @pl.when(i == O6)
        def _():
            for t in range(BLOCKS):
                hid_copy(t).wait()

        stage(O6, e6)
        stage(O7, e7)
        stage(O6B, e6b)
        stage(O6 - 2, w_start)
        stage(O8, e8)
        for b in range(FIN_PER):
            t = (i - (SLICES + O6B - 1)) * FIN_PER + b

            @pl.when((t >= 0) & (t < BLOCKS))
            def _():
                finish(t)

        return carry

    lax.fori_loop(0, SLICES + O8, step, 0)

    cp_gd = pltpu.make_async_copy(gd, gd_ref, osem.at[0, 0])
    cp_gd.start()
    for t in range(BLOCKS):
        for cp in out_copies(t):
            cp.wait()
    cp_gd.wait()


def body(grad_out, gate_act, up_act, down_weight):
    token_total = grad_out.shape[0] * lax.axis_size("tp") * lax.axis_size("dp")
    bf16 = jnp.bfloat16
    any_spec = pl.BlockSpec(memory_space=pl.ANY)
    dma = pltpu.SemaphoreType.DMA
    return pl.pallas_call(
        functools.partial(kernel, 1.0 / math.sqrt(token_total)),
        out_shape=(jax.ShapeDtypeStruct((GROUP, FF), bf16), jax.ShapeDtypeStruct((GROUP, FF), bf16),
                   jax.ShapeDtypeStruct((CHUNK, D), bf16)),
        in_specs=[any_spec] * 4,
        out_specs=(any_spec,) * 3,
        scratch_shapes=[
            pltpu.VMEM((2, SLICES, 16, CHUNK, W), bf16),
            pltpu.VMEM((4, 2, CHUNK, GROUP), bf16),
            pltpu.VMEM((4, CHUNK, GROUP), bf16),
            pltpu.VMEM((GROUP, FF), bf16),
            pltpu.VMEM((GROUP, FF), bf16),
            pltpu.VMEM((GROUP, FF), jnp.float32),
            pltpu.VMEM((3, 2, FF, W), bf16),
            pltpu.VMEM((SLICES, 4, CHUNK, 2 * W), bf16),
            pltpu.VMEM((SLICES, CHUNK, 2 * W), bf16),
            pltpu.VMEM((SLICES, CHUNK, 2 * W), bf16),
            pltpu.VMEM((SLICES, CHUNK, 2 * W), bf16),
            pltpu.VMEM((CHUNK // 2, HALF), bf16),
            pltpu.VMEM((CHUNK // 2, HALF), bf16),
            pltpu.VMEM((CHUNK, D), bf16),
            dma((SLICES, MSGS)), dma((SLICES, MSGS)),
            dma((BLOCKS,)), dma((BLOCKS,)), dma((1,)), dma((1,)),
            dma((3, 2)), dma((3,)), dma((3, BLOCKS)),
        ],
        compiler_params=pltpu.CompilerParams(
            collective_id=0, has_side_effects=True, vmem_limit_bytes=62 * 1024 * 1024),
        cost_estimate=pl.CostEstimate(flops=4 * FF * GROUP * D, bytes_accessed=24 * 1024 * 1024,
                                      transcendentals=GROUP * FF * 2),
    )(grad_out, gate_act, up_act, down_weight)


def solution(mesh):
    return jax.shard_map(
        body,
        mesh=mesh,
        in_specs=(P(("dp", "tp"), None), P("dp", "tp"), P("dp", "tp"), P("tp", None)),
        out_specs=(P("dp", "tp"), P("dp", "tp"), P(("tp", "dp"), None)),
        check_vma=False,
    )
```

```python
import functools
import math

import jax
import jax.numpy as jnp
from jax import lax
from jax.experimental import pallas as pl
from jax.experimental.pallas import tpu as pltpu
from jax.sharding import PartitionSpec as P

MESH = pl.DeviceIdType.MESH
D = 8192
FF = 896
GROUP = 896
CHUNK = 112
SLICES = 16
W = D // 2 // SLICES
HALF = D // 2
MSGS = 15
BLK = 128
BLOCKS = GROUP // BLK
HID_PER = 1
FIN_PER = 2
O1, O2, O3, O4, O5, O6, O6B, O7, O8 = 0, 2, 4, 6, 8, 9, 9, 11, 13


def kernel(scale, go_ref, gate_ref, up_ref, w_ref, gg_ref, gu_ref, gd_ref,
           g, ht, ho, gate, up, acc, wbuf, part, ra, rb, rc, mine, theirs, gd,
           ss, rs, hs, hr, ls, lr, wsem, lsem, osem):
    tp, dp = lax.axis_index("tp"), lax.axis_index("dp")
    x, y, c = tp // 4, dp // 2, tp % 2
    zh, zl = dp % 2, (tp // 2) % 2
    z = zh * 2 + zl
    f32 = jnp.float32

    def at(xx, yy, zz, cc):
        return {"dp": yy * 2 + zz // 2, "tp": xx * 4 + (zz % 2) * 2 + cc}

    def kind(k):
        return jnp.where((k % 2 == 0) & (k >= 2), 1, 0)

    def pq(k):
        b = kind(k)
        return x + b * (z - x), z + b * (x - z)

    def q_dev(k, d):
        b = kind(k)
        return at((x + b * d + 4) % 4, y, (z + (1 - b) * d + 4) % 4, c)

    def p_dev(k, d):
        b = kind(k)
        return at((x + (1 - b) * d + 4) % 4, y, (z + b * d + 4) % 4, c)

    def y_dev(d):
        return at(x, (y + d + 4) % 4, z, c)

    sib = at(x, y, z, 1 - c)
    partner = at(x, y, (z + 2) % 4, c)

    def rcopy(ref, k, m, dev):
        return pltpu.make_async_remote_copy(
            src_ref=ref, dst_ref=ref, send_sem=ss.at[k, m], recv_sem=rs.at[k, m],
            device_id=dev, device_id_type=MESH)

    def one(h, k, p, q):
        return g.at[h, k, pl.ds(((p + 4) % 4) * 4 + (q + 4) % 4, 1)]

    def group(h, k, p):
        return g.at[h, k, pl.ds(((p + 4) % 4) * 4, 4)]

    def half(h, k, p, j):
        return g.at[h, k, pl.ds(((p + 4) % 4) * 4 + 2 * j, 2)]

    def sgn(k):
        return 1 - 2 * ((k // 2) % 2)

    def ysgn(k):
        return 1 - 2 * (k % 2)

    cp_gate = pltpu.make_async_copy(gate_ref, gate, lsem.at[0])
    cp_up = pltpu.make_async_copy(up_ref, up, lsem.at[1])
    cp_mine = pltpu.make_async_copy(go_ref.at[:, pl.ds(pl.multiple_of(c * HALF, HALF), HALF)], mine, lsem.at[2])
    cp_mine.start()
    cp_gate.start()
    cp_up.start()

    barrier = pltpu.get_barrier_semaphore()
    for dev in (at((x + 1) % 4, y, z, c), at((x + 3) % 4, y, z, c), at(x, y, (z + 1) % 4, c),
                at(x, y, (z + 3) % 4, c), y_dev(1), y_dev(-1), sib, partner):
        pl.semaphore_signal(barrier, inc=1, device_id=dev, device_id_type=MESH)
    pl.semaphore_wait(barrier, 8)

    cp_sib = pltpu.make_async_remote_copy(
        src_ref=go_ref.at[:, pl.ds(pl.multiple_of((1 - c) * HALF, HALF), HALF)], dst_ref=theirs,
        send_sem=ls.at[0], recv_sem=lr.at[0], device_id=sib, device_id_type=MESH)
    cp_sib.start()
    acc[...] = jnp.zeros_like(acc)
    cp_mine.wait()
    cp_sib.wait()

    def hid_copy(t):
        at_t = pl.ds(pl.multiple_of(t * BLK, BLK), BLK)
        return pltpu.make_async_remote_copy(
            src_ref=ht.at[:, 1 - zh, :, at_t], dst_ref=ho.at[:, :, at_t],
            send_sem=hs.at[t], recv_sem=hr.at[t], device_id=partner, device_id_type=MESH)

    def w_copy(k, h):
        cols = pl.ds(pl.multiple_of(h * HALF + k * W, W), W)
        return pltpu.make_async_copy(w_ref.at[:, cols], wbuf.at[k % 3, h], wsem.at[k % 3, h])

    def w_start(k):
        for h in range(2):
            w_copy(k, h).start()

    def e1(k):
        p, q = pq(k)
        cols = pl.ds(pl.multiple_of(k * W, W), W)
        a, b = mine[:, cols], theirs[:, cols]
        first, last = jnp.where(c == 0, a, b), jnp.where(c == 0, b, a)
        g[c, k, p * 4 + q] = jnp.concatenate([first, last], axis=0)
        rcopy(one(c, k, p, q), k, 0, q_dev(k, 1)).start()
        rcopy(one(c, k, p, q), k, 1, q_dev(k, -1)).start()

    def e2(k):
        p, q = pq(k)
        rcopy(one(c, k, p, q - 1), k, 0, q_dev(k, 1)).wait_recv()
        rcopy(one(c, k, p, q + 1), k, 1, q_dev(k, 1)).wait_recv()
        s = sgn(k)
        rcopy(one(c, k, p, q - s), k, 2, q_dev(k, s)).start()

    def e3(k):
        p, q = pq(k)
        rcopy(one(c, k, p, q + 2), k, 2, q_dev(k, 1)).wait_recv()
        rcopy(group(c, k, p), k, 3, p_dev(k, 1)).start()
        rcopy(group(c, k, p), k, 4, p_dev(k, -1)).start()
        rcopy(group(c, k, p), k, 7, sib).start()

    def e4(k):
        p, q = pq(k)
        rcopy(group(c, k, p - 1), k, 3, p_dev(k, 1)).wait_recv()
        rcopy(half(c, k, p - 1, 0), k, 5, p_dev(k, 1)).start()
        rcopy(group(c, k, p - 1), k, 8, sib).start()
        rcopy(group(c, k, p + 1), k, 4, p_dev(k, 1)).wait_recv()
        rcopy(half(c, k, p + 1, 1), k, 6, p_dev(k, -1)).start()
        rcopy(group(c, k, p + 1), k, 9, sib).start()

    def e5(k):
        p, q = pq(k)
        rcopy(half(c, k, p + 2, 0), k, 5, p_dev(k, 1)).wait_recv()
        rcopy(half(c, k, p + 2, 0), k, 10, sib).start()
        rcopy(half(c, k, p + 2, 1), k, 6, p_dev(k, 1)).wait_recv()
        rcopy(half(c, k, p + 2, 1), k, 11, sib).start()

    def rows(h, k, zz):
        b = kind(k)
        blocks = []
        for j in range(8):
            xj, zj = j // 2, zz * 2 + j % 2
            pos = (1 - b) * (xj * 4 + zj) + b * (zj * 4 + xj)
            blocks.append(g[h, k, pos])
        return jnp.concatenate(blocks, axis=0)

    def y_copy(k, src, dst, m, d):
        return pltpu.make_async_remote_copy(
            src_ref=src, dst_ref=dst, send_sem=ss.at[k, m], recv_sem=rs.at[k, m],
            device_id=y_dev(d), device_id_type=MESH)

    def blk(k, d):
        return part.at[k, (y + d + 4) % 4]

    def e6(k):
        p, q = pq(k)
        rcopy(group(1 - c, k, p), k, 7, sib).wait_recv()
        rcopy(group(1 - c, k, p - 1), k, 8, sib).wait_recv()
        rcopy(group(1 - c, k, p + 1), k, 9, sib).wait_recv()
        rcopy(half(1 - c, k, p + 2, 0), k, 10, sib).wait_recv()
        rcopy(half(1 - c, k, p + 2, 1), k, 11, sib).wait_recv()
        for h in range(2):
            own = ht[:, zh].reshape(FF // 2, GROUP)
            dw = jnp.dot(own, rows(h, k, zh), preferred_element_type=f32)
            dw += jnp.dot(ho[...].reshape(FF // 2, GROUP), rows(h, k, 1 - zh), preferred_element_type=f32)
            part[k, :, :, h * W:(h + 1) * W] = dw.astype(jnp.bfloat16).reshape(4, CHUNK, W)
        s = ysgn(k)
        y_copy(k, blk(k, 2), ra.at[k], 12, s).start()
        y_copy(k, blk(k, -s), rc.at[k], 14, -s).start()

    def e6b(k):
        for h in range(2):
            w_copy(k, h).wait()
        total = acc[...]
        for h in range(2):
            total += lax.dot_general(rows(h, k, zh), wbuf[k % 3, h], (((1,), (1,)), ((), ())),
                                     preferred_element_type=f32)
        acc[...] = total

    def e7(k):
        s = ysgn(k)
        y_copy(k, blk(k, 2), ra.at[k], 12, s).wait_recv()
        mid = (y + s + 4) % 4
        part[k, mid] = (part[k, mid].astype(f32) + ra[k].astype(f32)).astype(jnp.bfloat16)
        y_copy(k, blk(k, s), rb.at[k], 13, s).start()

    def e8(k):
        s = ysgn(k)
        p, q = pq(k)
        y_copy(k, blk(k, s), rb.at[k], 13, s).wait_recv()
        y_copy(k, blk(k, -s), rc.at[k], 14, -s).wait_recv()
        total = part[k, y].astype(f32) + rb[k].astype(f32) + rc[k].astype(f32)
        total = (total * scale).astype(jnp.bfloat16)
        for h in range(2):
            gd[:, pl.ds(pl.multiple_of(h * HALF + k * W, W), W)] = total[:, h * W:(h + 1) * W]
        rcopy(one(c, k, p, q), k, 0, sib).wait_send()
        rcopy(one(c, k, p, q), k, 1, sib).wait_send()
        rcopy(one(c, k, p, q - sgn(k)), k, 2, sib).wait_send()
        rcopy(group(c, k, p), k, 3, sib).wait_send()
        rcopy(group(c, k, p), k, 4, sib).wait_send()
        rcopy(half(c, k, p - 1, 0), k, 5, sib).wait_send()
        rcopy(half(c, k, p + 1, 1), k, 6, sib).wait_send()
        rcopy(group(c, k, p), k, 7, sib).wait_send()
        rcopy(group(c, k, p - 1), k, 8, sib).wait_send()
        rcopy(group(c, k, p + 1), k, 9, sib).wait_send()
        rcopy(half(c, k, p + 2, 0), k, 10, sib).wait_send()
        rcopy(half(c, k, p + 2, 1), k, 11, sib).wait_send()
        y_copy(k, blk(k, 2), ra.at[k], 12, s).wait_send()
        y_copy(k, blk(k, s), rb.at[k], 13, s).wait_send()
        y_copy(k, blk(k, -s), rc.at[k], 14, -s).wait_send()

    def hidden_block(t):
        at_t = pl.ds(pl.multiple_of(t * BLK, BLK), BLK)
        gv, uv = gate[at_t, :].astype(f32), up[at_t, :].astype(f32)
        hid = (gv * jax.nn.sigmoid(gv) * uv).T.astype(jnp.bfloat16)
        ht[:, :, :, at_t] = hid.reshape(4, 2, CHUNK, BLK)
        hid_copy(t).start()

    def out_copies(t):
        at_t = pl.ds(pl.multiple_of(t * BLK, BLK), BLK)
        return (pltpu.make_async_copy(gate.at[at_t, :], gg_ref.at[at_t, :], osem.at[1, t]),
                pltpu.make_async_copy(up.at[at_t, :], gu_ref.at[at_t, :], osem.at[2, t]))

    def finish(t):
        at_t = pl.ds(pl.multiple_of(t * BLK, BLK), BLK)
        gv, uv, gh = gate[at_t, :].astype(f32), up[at_t, :].astype(f32), acc[at_t, :]
        sq = jax.nn.sigmoid(gv)
        gate[at_t, :] = (gh * uv * sq * (1.0 + gv * (1.0 - sq))).astype(jnp.bfloat16)
        up[at_t, :] = (gh * gv * sq).astype(jnp.bfloat16)
        for cp in out_copies(t):
            cp.start()

    def step(i, carry):
        def stage(off, fn):
            k = i - off

            @pl.when((k >= 0) & (k < SLICES))
            def _():
                fn(k)

        stage(O2, e2)
        stage(O1, e1)
        stage(O3, e3)

        @pl.when(i == 0)
        def _():
            cp_gate.wait()
            cp_up.wait()

        for b in range(HID_PER):
            t = i * HID_PER + b

            @pl.when(t < BLOCKS)
            def _():
                hidden_block(t)

        stage(O4, e4)
        stage(O5, e5)

        @pl.when(i == O6)
        def _():
            for t in range(BLOCKS):
                hid_copy(t).wait()

        stage(O6, e6)
        stage(O7, e7)
        stage(O6B, e6b)
        stage(O6 - 2, w_start)
        stage(O8, e8)
        for b in range(FIN_PER):
            t = (i - (SLICES + O6B - 1)) * FIN_PER + b

            @pl.when((t >= 0) & (t < BLOCKS))
            def _():
                finish(t)

        return carry

    lax.fori_loop(0, SLICES + O8, step, 0)

    cp_gd = pltpu.make_async_copy(gd, gd_ref, osem.at[0, 0])
    cp_gd.start()
    for t in range(BLOCKS):
        for cp in out_copies(t):
            cp.wait()
    cp_gd.wait()


def body(grad_out, gate_act, up_act, down_weight):
    token_total = grad_out.shape[0] * lax.axis_size("tp") * lax.axis_size("dp")
    bf16 = jnp.bfloat16
    any_spec = pl.BlockSpec(memory_space=pl.ANY)
    dma = pltpu.SemaphoreType.DMA
    return pl.pallas_call(
        functools.partial(kernel, 1.0 / math.sqrt(token_total)),
        out_shape=(jax.ShapeDtypeStruct((GROUP, FF), bf16), jax.ShapeDtypeStruct((GROUP, FF), bf16),
                   jax.ShapeDtypeStruct((CHUNK, D), bf16)),
        in_specs=[any_spec] * 4,
        out_specs=(any_spec,) * 3,
        scratch_shapes=[
            pltpu.VMEM((2, SLICES, 16, CHUNK, W), bf16),
            pltpu.VMEM((4, 2, CHUNK, GROUP), bf16),
            pltpu.VMEM((4, CHUNK, GROUP), bf16),
            pltpu.VMEM((GROUP, FF), bf16),
            pltpu.VMEM((GROUP, FF), bf16),
            pltpu.VMEM((GROUP, FF), jnp.float32),
            pltpu.VMEM((3, 2, FF, W), bf16),
            pltpu.VMEM((SLICES, 4, CHUNK, 2 * W), bf16),
            pltpu.VMEM((SLICES, CHUNK, 2 * W), bf16),
            pltpu.VMEM((SLICES, CHUNK, 2 * W), bf16),
            pltpu.VMEM((SLICES, CHUNK, 2 * W), bf16),
            pltpu.VMEM((CHUNK // 2, HALF), bf16),
            pltpu.VMEM((CHUNK // 2, HALF), bf16),
            pltpu.VMEM((CHUNK, D), bf16),
            dma((SLICES, MSGS)), dma((SLICES, MSGS)),
            dma((BLOCKS,)), dma((BLOCKS,)), dma((1,)), dma((1,)),
            dma((3, 2)), dma((3,)), dma((3, BLOCKS)),
        ],
        compiler_params=pltpu.CompilerParams(
            collective_id=0, has_side_effects=True, vmem_limit_bytes=62 * 1024 * 1024),
        cost_estimate=pl.CostEstimate(flops=4 * FF * GROUP * D, bytes_accessed=24 * 1024 * 1024,
                                      transcendentals=GROUP * FF * 2),
    )(grad_out, gate_act, up_act, down_weight)


def solution(mesh):
    return jax.shard_map(
        body,
        mesh=mesh,
        in_specs=(P(("dp", "tp"), None), P("dp", "tp"), P("dp", "tp"), P("tp", None)),
        out_specs=(P("dp", "tp"), P("dp", "tp"), P(("tp", "dp"), None)),
        check_vma=False,
    )
```

```python
import functools
import math

import jax
import jax.numpy as jnp
from jax import lax
from jax.experimental import pallas as pl
from jax.experimental.pallas import tpu as pltpu
from jax.sharding import PartitionSpec as P

MESH = pl.DeviceIdType.MESH
D = 8192
FF = 896
GROUP = 896
CHUNK = 112
SLICES = 16
W = D // 2 // SLICES
HALF = D // 2
MSGS = 15
BLK = 128
BLOCKS = GROUP // BLK
HID_PER = 1
PIECES = 4
FIN_PER = 2
O1, O2, O3, O4, O5, O6, O6B, O7, O8 = 0, 2, 4, 6, 8, 9, 9, 11, 13


def kernel(scale, go_ref, gate_ref, up_ref, w_ref, gg_ref, gu_ref, gd_ref,
           g, ht, ho, gate, up, acc, wbuf, part, ra, rb, rc, mine, theirs, gd,
           ss, rs, hs, hr, ls, lr, wsem, lsem, osem, gsem):
    tp, dp = lax.axis_index("tp"), lax.axis_index("dp")
    x, y, c = tp // 4, dp // 2, tp % 2
    zh, zl = dp % 2, (tp // 2) % 2
    z = zh * 2 + zl
    f32 = jnp.float32

    def at(xx, yy, zz, cc):
        return {"dp": yy * 2 + zz // 2, "tp": xx * 4 + (zz % 2) * 2 + cc}

    def kind(k):
        return jnp.where((k % 2 == 0) & (k >= 2), 1, 0)

    def pq(k):
        b = kind(k)
        return x + b * (z - x), z + b * (x - z)

    def q_dev(k, d):
        b = kind(k)
        return at((x + b * d + 4) % 4, y, (z + (1 - b) * d + 4) % 4, c)

    def p_dev(k, d):
        b = kind(k)
        return at((x + (1 - b) * d + 4) % 4, y, (z + b * d + 4) % 4, c)

    def y_dev(d):
        return at(x, (y + d + 4) % 4, z, c)

    sib = at(x, y, z, 1 - c)
    partner = at(x, y, (z + 2) % 4, c)

    def rcopy(ref, k, m, dev):
        return pltpu.make_async_remote_copy(
            src_ref=ref, dst_ref=ref, send_sem=ss.at[k, m], recv_sem=rs.at[k, m],
            device_id=dev, device_id_type=MESH)

    def one(h, k, p, q):
        return g.at[h, k, pl.ds(((p + 4) % 4) * 4 + (q + 4) % 4, 1)]

    def group(h, k, p):
        return g.at[h, k, pl.ds(((p + 4) % 4) * 4, 4)]

    def half(h, k, p, j):
        return g.at[h, k, pl.ds(((p + 4) % 4) * 4 + 2 * j, 2)]

    def sgn(k):
        return 1 - 2 * ((k // 2) % 2)

    def ysgn(k):
        return 1 - 2 * (k % 2)

    cp_gate = pltpu.make_async_copy(gate_ref, gate, lsem.at[0])
    cp_up = pltpu.make_async_copy(up_ref, up, lsem.at[1])
    part_w = HALF // PIECES

    def mine_copy(n):
        src = go_ref.at[:, pl.ds(pl.multiple_of(c * HALF + n * part_w, part_w), part_w)]
        return pltpu.make_async_copy(src, mine.at[:, pl.ds(pl.multiple_of(n * part_w, part_w), part_w)], lsem.at[2 + n])

    def theirs_copy(n):
        src = go_ref.at[:, pl.ds(pl.multiple_of((1 - c) * HALF + n * part_w, part_w), part_w)]
        return pltpu.make_async_remote_copy(
            src_ref=src, dst_ref=theirs.at[:, pl.ds(pl.multiple_of(n * part_w, part_w), part_w)],
            send_sem=ls.at[n], recv_sem=lr.at[n], device_id=sib, device_id_type=MESH)

    for n in range(PIECES):
        mine_copy(n).start()
    cp_gate.start()
    cp_up.start()

    barrier = pltpu.get_barrier_semaphore()
    for dev in (at((x + 1) % 4, y, z, c), at((x + 3) % 4, y, z, c), at(x, y, (z + 1) % 4, c),
                at(x, y, (z + 3) % 4, c), y_dev(1), y_dev(-1), sib, partner):
        pl.semaphore_signal(barrier, inc=1, device_id=dev, device_id_type=MESH)
    pl.semaphore_wait(barrier, 8)

    for n in range(PIECES):
        theirs_copy(n).start()
    acc[...] = jnp.zeros_like(acc)

    def hid_copy(t):
        at_t = pl.ds(pl.multiple_of(t * BLK, BLK), BLK)
        return pltpu.make_async_remote_copy(
            src_ref=ht.at[:, 1 - zh, :, at_t], dst_ref=ho.at[:, :, at_t],
            send_sem=hs.at[t], recv_sem=hr.at[t], device_id=partner, device_id_type=MESH)

    def w_copy(k, h):
        cols = pl.ds(pl.multiple_of(h * HALF + k * W, W), W)
        return pltpu.make_async_copy(w_ref.at[:, cols], wbuf.at[k % 3, h], wsem.at[k % 3, h])

    def w_start(k):
        for h in range(2):
            w_copy(k, h).start()

    def e1(k):
        p, q = pq(k)

        @pl.when(k % (SLICES // PIECES) == 0)
        def _():
            n = k // (SLICES // PIECES)
            mine_copy(n).wait()
            theirs_copy(n).wait()

        cols = pl.ds(pl.multiple_of(k * W, W), W)
        a, b = mine[:, cols], theirs[:, cols]
        first, last = jnp.where(c == 0, a, b), jnp.where(c == 0, b, a)
        g[c, k, p * 4 + q] = jnp.concatenate([first, last], axis=0)
        rcopy(one(c, k, p, q), k, 0, q_dev(k, 1)).start()
        rcopy(one(c, k, p, q), k, 1, q_dev(k, -1)).start()

    def e2(k):
        p, q = pq(k)
        rcopy(one(c, k, p, q - 1), k, 0, q_dev(k, 1)).wait_recv()
        rcopy(one(c, k, p, q + 1), k, 1, q_dev(k, 1)).wait_recv()
        s = sgn(k)
        rcopy(one(c, k, p, q - s), k, 2, q_dev(k, s)).start()

    def e3(k):
        p, q = pq(k)
        rcopy(one(c, k, p, q + 2), k, 2, q_dev(k, 1)).wait_recv()
        rcopy(group(c, k, p), k, 3, p_dev(k, 1)).start()
        rcopy(group(c, k, p), k, 4, p_dev(k, -1)).start()
        rcopy(group(c, k, p), k, 7, sib).start()

    def e4(k):
        p, q = pq(k)
        rcopy(group(c, k, p - 1), k, 3, p_dev(k, 1)).wait_recv()
        rcopy(half(c, k, p - 1, 0), k, 5, p_dev(k, 1)).start()
        rcopy(group(c, k, p - 1), k, 8, sib).start()
        rcopy(group(c, k, p + 1), k, 4, p_dev(k, 1)).wait_recv()
        rcopy(half(c, k, p + 1, 1), k, 6, p_dev(k, -1)).start()
        rcopy(group(c, k, p + 1), k, 9, sib).start()

    def e5(k):
        p, q = pq(k)
        rcopy(half(c, k, p + 2, 0), k, 5, p_dev(k, 1)).wait_recv()
        rcopy(half(c, k, p + 2, 0), k, 10, sib).start()
        rcopy(half(c, k, p + 2, 1), k, 6, p_dev(k, 1)).wait_recv()
        rcopy(half(c, k, p + 2, 1), k, 11, sib).start()

    def rows(h, k, zz):
        b = kind(k)
        blocks = []
        for j in range(8):
            xj, zj = j // 2, zz * 2 + j % 2
            pos = (1 - b) * (xj * 4 + zj) + b * (zj * 4 + xj)
            blocks.append(g[h, k, pos])
        return jnp.concatenate(blocks, axis=0)

    def y_copy(k, src, dst, m, d):
        return pltpu.make_async_remote_copy(
            src_ref=src, dst_ref=dst, send_sem=ss.at[k, m], recv_sem=rs.at[k, m],
            device_id=y_dev(d), device_id_type=MESH)

    def blk(k, d):
        return part.at[k, (y + d + 4) % 4]

    def e6(k):
        p, q = pq(k)
        rcopy(group(1 - c, k, p), k, 7, sib).wait_recv()
        rcopy(group(1 - c, k, p - 1), k, 8, sib).wait_recv()
        rcopy(group(1 - c, k, p + 1), k, 9, sib).wait_recv()
        rcopy(half(1 - c, k, p + 2, 0), k, 10, sib).wait_recv()
        rcopy(half(1 - c, k, p + 2, 1), k, 11, sib).wait_recv()
        for h in range(2):
            own = ht[:, zh].reshape(FF // 2, GROUP)
            dw = jnp.dot(own, rows(h, k, zh), preferred_element_type=f32)
            dw += jnp.dot(ho[...].reshape(FF // 2, GROUP), rows(h, k, 1 - zh), preferred_element_type=f32)
            part[k, :, :, h * W:(h + 1) * W] = dw.astype(jnp.bfloat16).reshape(4, CHUNK, W)
        s = ysgn(k)
        y_copy(k, blk(k, 2), ra.at[k], 12, s).start()
        y_copy(k, blk(k, -s), rc.at[k], 14, -s).start()

    def e6b(k):
        for h in range(2):
            w_copy(k, h).wait()
        total = acc[...]
        for h in range(2):
            total += lax.dot_general(rows(h, k, zh), wbuf[k % 3, h], (((1,), (1,)), ((), ())),
                                     preferred_element_type=f32)
        acc[...] = total

    def e7(k):
        s = ysgn(k)
        y_copy(k, blk(k, 2), ra.at[k], 12, s).wait_recv()
        mid = (y + s + 4) % 4
        part[k, mid] = (part[k, mid].astype(f32) + ra[k].astype(f32)).astype(jnp.bfloat16)
        y_copy(k, blk(k, s), rb.at[k], 13, s).start()

    def gd_copy(k, h):
        cols = pl.ds(pl.multiple_of(h * HALF + k * W, W), W)
        return pltpu.make_async_copy(gd.at[:, cols], gd_ref.at[:, cols], gsem.at[k, h])

    def e8(k):
        s = ysgn(k)
        p, q = pq(k)
        y_copy(k, blk(k, s), rb.at[k], 13, s).wait_recv()
        y_copy(k, blk(k, -s), rc.at[k], 14, -s).wait_recv()
        total = part[k, y].astype(f32) + rb[k].astype(f32) + rc[k].astype(f32)
        total = (total * scale).astype(jnp.bfloat16)
        for h in range(2):
            gd[:, pl.ds(pl.multiple_of(h * HALF + k * W, W), W)] = total[:, h * W:(h + 1) * W]
            gd_copy(k, h).start()
        rcopy(one(c, k, p, q), k, 0, sib).wait_send()
        rcopy(one(c, k, p, q), k, 1, sib).wait_send()
        rcopy(one(c, k, p, q - sgn(k)), k, 2, sib).wait_send()
        rcopy(group(c, k, p), k, 3, sib).wait_send()
        rcopy(group(c, k, p), k, 4, sib).wait_send()
        rcopy(half(c, k, p - 1, 0), k, 5, sib).wait_send()
        rcopy(half(c, k, p + 1, 1), k, 6, sib).wait_send()
        rcopy(group(c, k, p), k, 7, sib).wait_send()
        rcopy(group(c, k, p - 1), k, 8, sib).wait_send()
        rcopy(group(c, k, p + 1), k, 9, sib).wait_send()
        rcopy(half(c, k, p + 2, 0), k, 10, sib).wait_send()
        rcopy(half(c, k, p + 2, 1), k, 11, sib).wait_send()
        y_copy(k, blk(k, 2), ra.at[k], 12, s).wait_send()
        y_copy(k, blk(k, s), rb.at[k], 13, s).wait_send()
        y_copy(k, blk(k, -s), rc.at[k], 14, -s).wait_send()

    def hidden_block(t):
        at_t = pl.ds(pl.multiple_of(t * BLK, BLK), BLK)
        gv, uv = gate[at_t, :].astype(f32), up[at_t, :].astype(f32)
        hid = (gv * jax.nn.sigmoid(gv) * uv).T.astype(jnp.bfloat16)
        ht[:, :, :, at_t] = hid.reshape(4, 2, CHUNK, BLK)
        hid_copy(t).start()

    def out_copies(t):
        at_t = pl.ds(pl.multiple_of(t * BLK, BLK), BLK)
        return (pltpu.make_async_copy(gate.at[at_t, :], gg_ref.at[at_t, :], osem.at[1, t]),
                pltpu.make_async_copy(up.at[at_t, :], gu_ref.at[at_t, :], osem.at[2, t]))

    def finish(t):
        at_t = pl.ds(pl.multiple_of(t * BLK, BLK), BLK)
        gv, uv, gh = gate[at_t, :].astype(f32), up[at_t, :].astype(f32), acc[at_t, :]
        sq = jax.nn.sigmoid(gv)
        gate[at_t, :] = (gh * uv * sq * (1.0 + gv * (1.0 - sq))).astype(jnp.bfloat16)
        up[at_t, :] = (gh * gv * sq).astype(jnp.bfloat16)
        for cp in out_copies(t):
            cp.start()

    def step(i, carry):
        def stage(off, fn):
            k = i - off

            @pl.when((k >= 0) & (k < SLICES))
            def _():
                fn(k)

        stage(O2, e2)
        stage(O1, e1)
        stage(O3, e3)

        @pl.when(i == 0)
        def _():
            cp_gate.wait()
            cp_up.wait()

        for b in range(HID_PER):
            t = i * HID_PER + b

            @pl.when(t < BLOCKS)
            def _():
                hidden_block(t)

        stage(O4, e4)
        stage(O5, e5)

        @pl.when(i == O6)
        def _():
            for t in range(BLOCKS):
                hid_copy(t).wait()

        stage(O6, e6)
        stage(O7, e7)
        stage(O6B, e6b)
        stage(O6 - 2, w_start)
        stage(O8, e8)
        for b in range(FIN_PER):
            t = (i - (SLICES + O6B - 1)) * FIN_PER + b

            @pl.when((t >= 0) & (t < BLOCKS))
            def _():
                finish(t)

        return carry

    lax.fori_loop(0, SLICES + O8, step, 0)

    def gd_wait(k, carry):
        for h in range(2):
            gd_copy(k, h).wait()
        return carry

    lax.fori_loop(0, SLICES, gd_wait, 0)
    for t in range(BLOCKS):
        for cp in out_copies(t):
            cp.wait()


def body(grad_out, gate_act, up_act, down_weight):
    token_total = grad_out.shape[0] * lax.axis_size("tp") * lax.axis_size("dp")
    bf16 = jnp.bfloat16
    any_spec = pl.BlockSpec(memory_space=pl.ANY)
    dma = pltpu.SemaphoreType.DMA
    return pl.pallas_call(
        functools.partial(kernel, 1.0 / math.sqrt(token_total)),
        out_shape=(jax.ShapeDtypeStruct((GROUP, FF), bf16), jax.ShapeDtypeStruct((GROUP, FF), bf16),
                   jax.ShapeDtypeStruct((CHUNK, D), bf16)),
        in_specs=[any_spec] * 4,
        out_specs=(any_spec,) * 3,
        scratch_shapes=[
            pltpu.VMEM((2, SLICES, 16, CHUNK, W), bf16),
            pltpu.VMEM((4, 2, CHUNK, GROUP), bf16),
            pltpu.VMEM((4, CHUNK, GROUP), bf16),
            pltpu.VMEM((GROUP, FF), bf16),
            pltpu.VMEM((GROUP, FF), bf16),
            pltpu.VMEM((GROUP, FF), jnp.float32),
            pltpu.VMEM((3, 2, FF, W), bf16),
            pltpu.VMEM((SLICES, 4, CHUNK, 2 * W), bf16),
            pltpu.VMEM((SLICES, CHUNK, 2 * W), bf16),
            pltpu.VMEM((SLICES, CHUNK, 2 * W), bf16),
            pltpu.VMEM((SLICES, CHUNK, 2 * W), bf16),
            pltpu.VMEM((CHUNK // 2, HALF), bf16),
            pltpu.VMEM((CHUNK // 2, HALF), bf16),
            pltpu.VMEM((CHUNK, D), bf16),
            dma((SLICES, MSGS)), dma((SLICES, MSGS)),
            dma((BLOCKS,)), dma((BLOCKS,)), dma((PIECES,)), dma((PIECES,)),
            dma((3, 2)), dma((2 + PIECES,)), dma((3, BLOCKS)), dma((SLICES, 2)),
        ],
        compiler_params=pltpu.CompilerParams(
            collective_id=0, has_side_effects=True, vmem_limit_bytes=62 * 1024 * 1024),
        cost_estimate=pl.CostEstimate(flops=4 * FF * GROUP * D, bytes_accessed=24 * 1024 * 1024,
                                      transcendentals=GROUP * FF * 2),
    )(grad_out, gate_act, up_act, down_weight)


def solution(mesh):
    return jax.shard_map(
        body,
        mesh=mesh,
        in_specs=(P(("dp", "tp"), None), P("dp", "tp"), P("dp", "tp"), P("tp", None)),
        out_specs=(P("dp", "tp"), P("dp", "tp"), P(("tp", "dp"), None)),
        check_vma=False,
    )
```

```python
import functools
import math

import jax
import jax.numpy as jnp
from jax import lax
from jax.experimental import pallas as pl
from jax.experimental.pallas import tpu as pltpu
from jax.sharding import PartitionSpec as P

MESH = pl.DeviceIdType.MESH
D = 8192
FF = 896
GROUP = 896
CHUNK = 112
SLICES = 16
W = D // 2 // SLICES
HALF = D // 2
MSGS = 15
BLK = 128
BLOCKS = GROUP // BLK
HID_PER = 1
PIECES = 8
FIN_PER = 2
O1, O2, O3, O4, O5, O6, O6B, O7, O8 = 0, 2, 4, 6, 8, 9, 9, 11, 13


def kernel(scale, go_ref, gate_ref, up_ref, w_ref, gg_ref, gu_ref, gd_ref,
           g, ht, ho, gate, up, acc, wbuf, part, ra, rb, rc, mine, theirs, gd,
           ss, rs, hs, hr, ls, lr, wsem, lsem, osem, gsem):
    tp, dp = lax.axis_index("tp"), lax.axis_index("dp")
    x, y, c = tp // 4, dp // 2, tp % 2
    zh, zl = dp % 2, (tp // 2) % 2
    z = zh * 2 + zl
    f32 = jnp.float32

    def at(xx, yy, zz, cc):
        return {"dp": yy * 2 + zz // 2, "tp": xx * 4 + (zz % 2) * 2 + cc}

    def kind(k):
        return jnp.where((k % 2 == 0) & (k >= 2), 1, 0)

    def pq(k):
        b = kind(k)
        return x + b * (z - x), z + b * (x - z)

    def q_dev(k, d):
        b = kind(k)
        return at((x + b * d + 4) % 4, y, (z + (1 - b) * d + 4) % 4, c)

    def p_dev(k, d):
        b = kind(k)
        return at((x + (1 - b) * d + 4) % 4, y, (z + b * d + 4) % 4, c)

    def y_dev(d):
        return at(x, (y + d + 4) % 4, z, c)

    sib = at(x, y, z, 1 - c)
    partner = at(x, y, (z + 2) % 4, c)

    def rcopy(ref, k, m, dev):
        return pltpu.make_async_remote_copy(
            src_ref=ref, dst_ref=ref, send_sem=ss.at[k, m], recv_sem=rs.at[k, m],
            device_id=dev, device_id_type=MESH)

    def one(h, k, p, q):
        return g.at[h, k, pl.ds(((p + 4) % 4) * 4 + (q + 4) % 4, 1)]

    def group(h, k, p):
        return g.at[h, k, pl.ds(((p + 4) % 4) * 4, 4)]

    def half(h, k, p, j):
        return g.at[h, k, pl.ds(((p + 4) % 4) * 4 + 2 * j, 2)]

    def sgn(k):
        return 1 - 2 * ((k // 2) % 2)

    def ysgn(k):
        return 1 - 2 * (k % 2)

    cp_gate = pltpu.make_async_copy(gate_ref, gate, lsem.at[0])
    cp_up = pltpu.make_async_copy(up_ref, up, lsem.at[1])
    part_w = HALF // PIECES

    def mine_copy(n):
        src = go_ref.at[:, pl.ds(pl.multiple_of(c * HALF + n * part_w, part_w), part_w)]
        return pltpu.make_async_copy(src, mine.at[:, pl.ds(pl.multiple_of(n * part_w, part_w), part_w)], lsem.at[2 + n])

    def theirs_copy(n):
        src = go_ref.at[:, pl.ds(pl.multiple_of((1 - c) * HALF + n * part_w, part_w), part_w)]
        return pltpu.make_async_remote_copy(
            src_ref=src, dst_ref=theirs.at[:, pl.ds(pl.multiple_of(n * part_w, part_w), part_w)],
            send_sem=ls.at[n], recv_sem=lr.at[n], device_id=sib, device_id_type=MESH)

    for n in range(PIECES):
        mine_copy(n).start()
    cp_gate.start()
    cp_up.start()

    barrier = pltpu.get_barrier_semaphore()
    for dev in (at((x + 1) % 4, y, z, c), at((x + 3) % 4, y, z, c), at(x, y, (z + 1) % 4, c),
                at(x, y, (z + 3) % 4, c), y_dev(1), y_dev(-1), sib, partner):
        pl.semaphore_signal(barrier, inc=1, device_id=dev, device_id_type=MESH)
    pl.semaphore_wait(barrier, 8)

    for n in range(PIECES):
        theirs_copy(n).start()
    acc[...] = jnp.zeros_like(acc)

    def hid_copy(t):
        at_t = pl.ds(pl.multiple_of(t * BLK, BLK), BLK)
        return pltpu.make_async_remote_copy(
            src_ref=ht.at[:, 1 - zh, :, at_t], dst_ref=ho.at[:, :, at_t],
            send_sem=hs.at[t], recv_sem=hr.at[t], device_id=partner, device_id_type=MESH)

    def w_copy(k, h):
        cols = pl.ds(pl.multiple_of(h * HALF + k * W, W), W)
        return pltpu.make_async_copy(w_ref.at[:, cols], wbuf.at[k % 3, h], wsem.at[k % 3, h])

    def w_start(k):
        for h in range(2):
            w_copy(k, h).start()

    def e1(k):
        p, q = pq(k)

        @pl.when(k % (SLICES // PIECES) == 0)
        def _():
            n = k // (SLICES // PIECES)
            mine_copy(n).wait()
            theirs_copy(n).wait()

        cols = pl.ds(pl.multiple_of(k * W, W), W)
        a, b = mine[:, cols], theirs[:, cols]
        first, last = jnp.where(c == 0, a, b), jnp.where(c == 0, b, a)
        g[c, k, p * 4 + q] = jnp.concatenate([first, last], axis=0)
        rcopy(one(c, k, p, q), k, 0, q_dev(k, 1)).start()
        rcopy(one(c, k, p, q), k, 1, q_dev(k, -1)).start()

    def e2(k):
        p, q = pq(k)
        rcopy(one(c, k, p, q - 1), k, 0, q_dev(k, 1)).wait_recv()
        rcopy(one(c, k, p, q + 1), k, 1, q_dev(k, 1)).wait_recv()
        s = sgn(k)
        rcopy(one(c, k, p, q - s), k, 2, q_dev(k, s)).start()

    def e3(k):
        p, q = pq(k)
        rcopy(one(c, k, p, q + 2), k, 2, q_dev(k, 1)).wait_recv()
        rcopy(group(c, k, p), k, 3, p_dev(k, 1)).start()
        rcopy(group(c, k, p), k, 4, p_dev(k, -1)).start()
        rcopy(group(c, k, p), k, 7, sib).start()

    def e4(k):
        p, q = pq(k)
        rcopy(group(c, k, p - 1), k, 3, p_dev(k, 1)).wait_recv()
        rcopy(half(c, k, p - 1, 0), k, 5, p_dev(k, 1)).start()
        rcopy(group(c, k, p - 1), k, 8, sib).start()
        rcopy(group(c, k, p + 1), k, 4, p_dev(k, 1)).wait_recv()
        rcopy(half(c, k, p + 1, 1), k, 6, p_dev(k, -1)).start()
        rcopy(group(c, k, p + 1), k, 9, sib).start()

    def e5(k):
        p, q = pq(k)
        rcopy(half(c, k, p + 2, 0), k, 5, p_dev(k, 1)).wait_recv()
        rcopy(half(c, k, p + 2, 0), k, 10, sib).start()
        rcopy(half(c, k, p + 2, 1), k, 6, p_dev(k, 1)).wait_recv()
        rcopy(half(c, k, p + 2, 1), k, 11, sib).start()

    def rows(h, k, zz):
        b = kind(k)
        blocks = []
        for j in range(8):
            xj, zj = j // 2, zz * 2 + j % 2
            pos = (1 - b) * (xj * 4 + zj) + b * (zj * 4 + xj)
            blocks.append(g[h, k, pos])
        return jnp.concatenate(blocks, axis=0)

    def y_copy(k, src, dst, m, d):
        return pltpu.make_async_remote_copy(
            src_ref=src, dst_ref=dst, send_sem=ss.at[k, m], recv_sem=rs.at[k, m],
            device_id=y_dev(d), device_id_type=MESH)

    def blk(k, d):
        return part.at[k, (y + d + 4) % 4]

    def e6(k):
        p, q = pq(k)
        rcopy(group(1 - c, k, p), k, 7, sib).wait_recv()
        rcopy(group(1 - c, k, p - 1), k, 8, sib).wait_recv()
        rcopy(group(1 - c, k, p + 1), k, 9, sib).wait_recv()
        rcopy(half(1 - c, k, p + 2, 0), k, 10, sib).wait_recv()
        rcopy(half(1 - c, k, p + 2, 1), k, 11, sib).wait_recv()
        for h in range(2):
            own = ht[:, zh].reshape(FF // 2, GROUP)
            dw = jnp.dot(own, rows(h, k, zh), preferred_element_type=f32)
            dw += jnp.dot(ho[...].reshape(FF // 2, GROUP), rows(h, k, 1 - zh), preferred_element_type=f32)
            part[k, :, :, h * W:(h + 1) * W] = dw.astype(jnp.bfloat16).reshape(4, CHUNK, W)
        s = ysgn(k)
        y_copy(k, blk(k, 2), ra.at[k], 12, s).start()
        y_copy(k, blk(k, -s), rc.at[k], 14, -s).start()

    def e6b(k):
        for h in range(2):
            w_copy(k, h).wait()
        total = acc[...]
        for h in range(2):
            total += lax.dot_general(rows(h, k, zh), wbuf[k % 3, h], (((1,), (1,)), ((), ())),
                                     preferred_element_type=f32)
        acc[...] = total

    def e7(k):
        s = ysgn(k)
        y_copy(k, blk(k, 2), ra.at[k], 12, s).wait_recv()
        mid = (y + s + 4) % 4
        part[k, mid] = (part[k, mid].astype(f32) + ra[k].astype(f32)).astype(jnp.bfloat16)
        y_copy(k, blk(k, s), rb.at[k], 13, s).start()

    def gd_copy(k, h):
        cols = pl.ds(pl.multiple_of(h * HALF + k * W, W), W)
        return pltpu.make_async_copy(gd.at[:, cols], gd_ref.at[:, cols], gsem.at[k, h])

    def e8(k):
        s = ysgn(k)
        p, q = pq(k)
        y_copy(k, blk(k, s), rb.at[k], 13, s).wait_recv()
        y_copy(k, blk(k, -s), rc.at[k], 14, -s).wait_recv()
        total = part[k, y].astype(f32) + rb[k].astype(f32) + rc[k].astype(f32)
        total = (total * scale).astype(jnp.bfloat16)
        for h in range(2):
            gd[:, pl.ds(pl.multiple_of(h * HALF + k * W, W), W)] = total[:, h * W:(h + 1) * W]
            gd_copy(k, h).start()
        rcopy(one(c, k, p, q), k, 0, sib).wait_send()
        rcopy(one(c, k, p, q), k, 1, sib).wait_send()
        rcopy(one(c, k, p, q - sgn(k)), k, 2, sib).wait_send()
        rcopy(group(c, k, p), k, 3, sib).wait_send()
        rcopy(group(c, k, p), k, 4, sib).wait_send()
        rcopy(half(c, k, p - 1, 0), k, 5, sib).wait_send()
        rcopy(half(c, k, p + 1, 1), k, 6, sib).wait_send()
        rcopy(group(c, k, p), k, 7, sib).wait_send()
        rcopy(group(c, k, p - 1), k, 8, sib).wait_send()
        rcopy(group(c, k, p + 1), k, 9, sib).wait_send()
        rcopy(half(c, k, p + 2, 0), k, 10, sib).wait_send()
        rcopy(half(c, k, p + 2, 1), k, 11, sib).wait_send()
        y_copy(k, blk(k, 2), ra.at[k], 12, s).wait_send()
        y_copy(k, blk(k, s), rb.at[k], 13, s).wait_send()
        y_copy(k, blk(k, -s), rc.at[k], 14, -s).wait_send()

    def hidden_block(t):
        at_t = pl.ds(pl.multiple_of(t * BLK, BLK), BLK)
        gv, uv = gate[at_t, :].astype(f32), up[at_t, :].astype(f32)
        hid = (gv * jax.nn.sigmoid(gv) * uv).T.astype(jnp.bfloat16)
        ht[:, :, :, at_t] = hid.reshape(4, 2, CHUNK, BLK)
        hid_copy(t).start()

    def out_copies(t):
        at_t = pl.ds(pl.multiple_of(t * BLK, BLK), BLK)
        return (pltpu.make_async_copy(gate.at[at_t, :], gg_ref.at[at_t, :], osem.at[1, t]),
                pltpu.make_async_copy(up.at[at_t, :], gu_ref.at[at_t, :], osem.at[2, t]))

    def finish(t):
        at_t = pl.ds(pl.multiple_of(t * BLK, BLK), BLK)
        gv, uv, gh = gate[at_t, :].astype(f32), up[at_t, :].astype(f32), acc[at_t, :]
        sq = jax.nn.sigmoid(gv)
        gate[at_t, :] = (gh * uv * sq * (1.0 + gv * (1.0 - sq))).astype(jnp.bfloat16)
        up[at_t, :] = (gh * gv * sq).astype(jnp.bfloat16)
        for cp in out_copies(t):
            cp.start()

    def step(i, carry):
        def stage(off, fn):
            k = i - off

            @pl.when((k >= 0) & (k < SLICES))
            def _():
                fn(k)

        stage(O2, e2)
        stage(O1, e1)
        stage(O3, e3)

        @pl.when(i == 0)
        def _():
            cp_gate.wait()
            cp_up.wait()

        for b in range(HID_PER):
            t = i * HID_PER + b

            @pl.when(t < BLOCKS)
            def _():
                hidden_block(t)

        stage(O4, e4)
        stage(O5, e5)

        @pl.when(i == O6)
        def _():
            for t in range(BLOCKS):
                hid_copy(t).wait()

        stage(O6, e6)
        stage(O7, e7)
        stage(O6 - 2, w_start)
        stage(O8, e8)
        stage(O6B, e6b)
        for b in range(FIN_PER):
            t = (i - (SLICES + O6B - 1)) * FIN_PER + b

            @pl.when((t >= 0) & (t < BLOCKS))
            def _():
                finish(t)

        return carry

    lax.fori_loop(0, SLICES + O8, step, 0)

    def gd_wait(k, carry):
        for h in range(2):
            gd_copy(k, h).wait()
        return carry

    lax.fori_loop(0, SLICES, gd_wait, 0)
    for t in range(BLOCKS):
        for cp in out_copies(t):
            cp.wait()


def body(grad_out, gate_act, up_act, down_weight):
    token_total = grad_out.shape[0] * lax.axis_size("tp") * lax.axis_size("dp")
    bf16 = jnp.bfloat16
    any_spec = pl.BlockSpec(memory_space=pl.ANY)
    dma = pltpu.SemaphoreType.DMA
    return pl.pallas_call(
        functools.partial(kernel, 1.0 / math.sqrt(token_total)),
        out_shape=(jax.ShapeDtypeStruct((GROUP, FF), bf16), jax.ShapeDtypeStruct((GROUP, FF), bf16),
                   jax.ShapeDtypeStruct((CHUNK, D), bf16)),
        in_specs=[any_spec] * 4,
        out_specs=(any_spec,) * 3,
        scratch_shapes=[
            pltpu.VMEM((2, SLICES, 16, CHUNK, W), bf16),
            pltpu.VMEM((4, 2, CHUNK, GROUP), bf16),
            pltpu.VMEM((4, CHUNK, GROUP), bf16),
            pltpu.VMEM((GROUP, FF), bf16),
            pltpu.VMEM((GROUP, FF), bf16),
            pltpu.VMEM((GROUP, FF), jnp.float32),
            pltpu.VMEM((3, 2, FF, W), bf16),
            pltpu.VMEM((SLICES, 4, CHUNK, 2 * W), bf16),
            pltpu.VMEM((SLICES, CHUNK, 2 * W), bf16),
            pltpu.VMEM((SLICES, CHUNK, 2 * W), bf16),
            pltpu.VMEM((SLICES, CHUNK, 2 * W), bf16),
            pltpu.VMEM((CHUNK // 2, HALF), bf16),
            pltpu.VMEM((CHUNK // 2, HALF), bf16),
            pltpu.VMEM((CHUNK, D), bf16),
            dma((SLICES, MSGS)), dma((SLICES, MSGS)),
            dma((BLOCKS,)), dma((BLOCKS,)), dma((PIECES,)), dma((PIECES,)),
            dma((3, 2)), dma((2 + PIECES,)), dma((3, BLOCKS)), dma((SLICES, 2)),
        ],
        compiler_params=pltpu.CompilerParams(
            collective_id=0, has_side_effects=True, vmem_limit_bytes=62 * 1024 * 1024),
        cost_estimate=pl.CostEstimate(flops=4 * FF * GROUP * D, bytes_accessed=24 * 1024 * 1024,
                                      transcendentals=GROUP * FF * 2),
    )(grad_out, gate_act, up_act, down_weight)


def solution(mesh):
    return jax.shard_map(
        body,
        mesh=mesh,
        in_specs=(P(("dp", "tp"), None), P("dp", "tp"), P("dp", "tp"), P("tp", None)),
        out_specs=(P("dp", "tp"), P("dp", "tp"), P(("tp", "dp"), None)),
        check_vma=False,
    )
```
